256 devices in a mesh: group: 2 (over y_hi), fsdp: 16 (over y_lo, x, core), tp: 8 (over z).
Axes of the slice: x: 4, y: 4 (y_hi: 2, y_lo: 2; y = y_hi * 2 + y_lo), z: 8, core: 2. Of those that a mesh axis runs over, the one named last changes fastest.
Arguments:
- hidden: bfloat16 [2, 12288, 8192], P('group', 'fsdp', 'tp'), may hold values from -6 to 6
- cotangent: bfloat16 [12288, 2, 1024], P('fsdp', None, 'tp'), may hold values from -6 to 6
- queries: bfloat16 [12288, 8192], P('fsdp', 'tp'), may hold values from -160 to 160, as said below
- kv_cache: bfloat16 [6144, 2, 16, 1024], P('fsdp', None, None, 'tp'), may hold values from -7 to 7
- lengths: int32 [6144], P('fsdp'), may hold values from 2 to 16, as said below
- master: float32 [1024, 2, 8192], P('fsdp', None, 'tp'), may hold values from -4 to 4
- moment1: float32 [1024, 2, 8192], P('fsdp', None, 'tp'), may hold values from -1.5 to 1.5
- moment2: float32 [1024, 2, 8192], P('fsdp', None, 'tp'), may hold values from 0.002 to 0.02
Outputs:
- results: bfloat16 [2, 12288, 8192], P('group', 'fsdp', 'tp')
- new_master: float32 [1024, 2, 8192], P('fsdp', None, 'tp')
- new_first: float32 [1024, 2, 8192], P('fsdp', None, 'tp')
- new_second: float32 [1024, 2, 8192], P('fsdp', None, 'tp')
The draws below stay inside these ranges and needn't reach their ends.
Inputs may be any that keep to these rules, and one draw needn't show every extreme that they name: `queries`: token 2 * r + s is step s of rollout row r. `lengths`: the first of every 384 rows has all 16 positions in use.
All inputs are finite; a program needn't handle non-finite values.
Results may differ from the reference program's by a relative error of at most 0.0052.
Values may be sent and summed in bfloat16 or wider, within the bound.
No kernel may reach another device: no remote copies, remote signals or barrier semaphores. Data moves between devices by JAX's collectives and lax.ppermute only.
A program may use at most 192 MiB of HBM per device.

```python
import math
import jax
import jax.numpy as jnp
from jax import lax

D = 8192
KVW = 1024
HD = 128
TOK_DEV = 768
CACHE = 16
STEPS = 2
OPT_STEP = 100
TOKENS = 12288
ROWS = 6144


def shared_cache(key):
    return jax.random.truncated_normal(key, -6.0, 6.0, (ROWS, 2, CACHE, KVW), jnp.float32)


def draw_kv_cache(key, part):
    cached = shared_cache(key)
    return cached.astype(jnp.bfloat16)


def draw_queries(key, part):
    key = jax.random.fold_in(key, 2)
    values = jax.random.truncated_normal(key, -6.0, 6.0, (TOKENS, D), jnp.float32)
    return values.astype(jnp.bfloat16)


def draw_lengths(key, part):
    key = jax.random.fold_in(key, 3)
    drawn = jax.random.randint(key, (ROWS,), 2, CACHE + 1, dtype=jnp.int32)
    row_ids = jnp.arange(ROWS, dtype=jnp.int32)
    return jnp.where(row_ids % (TOK_DEV // STEPS) == 0, CACHE, drawn).astype(jnp.int32)


def with_spikes(values, rng, source, target, blocks, factor):
    owner, partner = [(jnp.arange(values.shape[dim]) // (values.shape[dim] // blocks)).reshape([-1 if axis == dim else 1 for axis in range(values.ndim)]) for dim in (source, target)]
    chosen = jax.random.permutation(rng, blocks)[partner]
    strong = (owner == chosen) | (owner == (partner + blocks // 2) % blocks)
    return jnp.where(strong, factor * values, values)


def level_of(rng, dims, split, smallest, largest):
    factor_of = 1.0
    for dim, parts in split:
        steps = jax.random.uniform(jax.random.fold_in(jax.random.fold_in(rng, 6), dim), (parts,), jnp.float32, smallest / len(split), largest / len(split))
        factor_of = factor_of * jnp.repeat(jnp.exp(steps), dims[dim] // parts).reshape((-1,) + (1,) * (len(dims) - 1 - dim))
    return factor_of


def normal_values(rng, extent, width, most, cuts=(), held_as=jnp.bfloat16):
    entries = jax.random.normal(rng, extent, jnp.float32) * width
    if len(cuts) > 0:
        entries = level_of(rng, extent, cuts, -0.22, 0.18) * entries
    return jnp.clip(entries, min=-most, max=most).astype(held_as)


def gaussian_with(key, shape, width, most, pieces, heavy, kind=jnp.bfloat16):
    result = width * jax.random.normal(key, shape, jnp.float32)
    if pieces:
        result = result * level_of(key, shape, pieces, -0.22, 0.18)
    return jnp.clip(with_spikes(result, jax.random.fold_in(key, 3), *heavy), -most, most).astype(kind)


def setup_inputs(seed: int = 0) -> dict:
    streams_of = jax.random.split(jax.random.key(seed), 9)
    return {
        "hidden": normal_values(streams_of[0], (2, TOKENS, D), 1.0, 6.0, ((0, 2), (1, 16), (2, 8))),
        "cotangent": gaussian_with(streams_of[1], (TOKENS, 2, KVW), 1.0, 6.0, ((0, 16), (2, 8)), (0, 2, 16, 2.0)),
        "queries": draw_queries(jax.random.fold_in(streams_of[8], 71), 0),
        "kv_cache": draw_kv_cache(jax.random.fold_in(streams_of[8], 71), 0),
        "lengths": draw_lengths(jax.random.fold_in(streams_of[8], 71), 0),
        "master": normal_values(streams_of[5], (KVW, 2, D), 1.0, 4.0, ((0, 16), (2, 8)), jnp.float32),
        "moment1": normal_values(streams_of[6], (KVW, 2, D), 0.1, 1.5, ((0, 16), (2, 8)), jnp.float32),
        "moment2": jnp.clip(jnp.exp(math.log(0.02) - 2.30258502 * jax.random.uniform(streams_of[7], (KVW, 2, D), jnp.float32) ** level_of(streams_of[7], (KVW, 2, D), ((0, 16), (2, 8)), -0.2, 0.2)), 0.002, 0.02),
    }


first_decay = 0.9
second_decay = 0.95
learn_rate = 0.15
weight_decay = 0.1
small_term = 1e-08

def attend_head(query, keys_old, values_old, keys_new, values_new, lengths):
    root = 1.0 / math.sqrt(HD)
    old_scores = jnp.einsum('rsgd,rpd->rsgp', query, keys_old) * root
    new_scores = jnp.einsum('rsgd,rjd->rsgj', query, keys_new) * root
    old_mask = (jnp.arange(CACHE, dtype=jnp.int32)[None, :] < lengths[:, None])[:, None, None, :]
    new_mask = (jnp.arange(STEPS)[None, :] <= jnp.arange(STEPS)[:, None])[None, :, None, :]
    top = jnp.maximum(lax.optimization_barrier(jnp.max(jnp.where(old_mask, old_scores, -jnp.inf), axis=-1, keepdims=True)), lax.optimization_barrier(jnp.max(jnp.where(new_mask, new_scores, -jnp.inf), axis=-1, keepdims=True)))
    old_exp = jnp.where(old_mask, jnp.exp(old_scores - top), 0.0)
    new_exp = jnp.where(new_mask, jnp.exp(new_scores - top), 0.0)
    total = lax.optimization_barrier(jnp.sum(old_exp, axis=-1, keepdims=True)) + lax.optimization_barrier(jnp.sum(new_exp, axis=-1, keepdims=True))
    old_probs = lax.optimization_barrier((old_exp / total).astype(jnp.bfloat16)).astype(jnp.float32)
    new_probs = lax.optimization_barrier((new_exp / total).astype(jnp.bfloat16)).astype(jnp.float32)
    return jnp.einsum('rsgp,rpd->rsgd', old_probs, values_old) + jnp.einsum('rsgj,rjd->rsgd', new_probs, values_new)

def reference(hidden, cotangent, queries, kv_cache, lengths, master, moment1, moment2):
    scale = 1.0 / math.sqrt(D)
    pairs = KVW * 2
    flat_cot = cotangent.transpose(0, 2, 1).reshape(TOKENS, pairs)
    old_weights = master.astype(jnp.bfloat16).reshape(pairs, D)
    input_grad = (jnp.dot(flat_cot, old_weights, preferred_element_type=jnp.float32) * scale).astype(jnp.bfloat16)
    gradient = (jnp.dot(flat_cot.T, hidden[0], preferred_element_type=jnp.float32) * scale).reshape(KVW, 2, D)
    new_first = first_decay * moment1 + (1.0 - first_decay) * gradient
    new_second = second_decay * moment2 + (1.0 - second_decay) * gradient * gradient
    first_hat = new_first / (1.0 - first_decay ** OPT_STEP)
    second_hat = new_second / (1.0 - second_decay ** OPT_STEP)
    new_master = master - learn_rate * (first_hat / (jnp.sqrt(second_hat) + small_term) + weight_decay * master)
    serving = new_master.astype(jnp.bfloat16).reshape(pairs, D)
    fresh = jnp.dot(hidden[1], serving.T, preferred_element_type=jnp.float32) * scale
    fresh = fresh.reshape(TOKENS, KVW, 2).transpose(0, 2, 1).astype(jnp.bfloat16)
    fresh_wide = lax.optimization_barrier(fresh).astype(jnp.float32)
    kv_heads = KVW // HD
    groups = D // KVW
    query = jnp.moveaxis(queries.astype(jnp.float32).reshape(ROWS, STEPS, kv_heads, groups, HD), 2, 0)
    cache_wide = kv_cache.astype(jnp.float32)
    keys_old = jnp.moveaxis(cache_wide[:, 0].reshape(ROWS, CACHE, kv_heads, HD), 2, 0)
    values_old = jnp.moveaxis(cache_wide[:, 1].reshape(ROWS, CACHE, kv_heads, HD), 2, 0)
    keys_new = jnp.moveaxis(fresh_wide[:, 0].reshape(ROWS, STEPS, kv_heads, HD), 2, 0)
    values_new = jnp.moveaxis(fresh_wide[:, 1].reshape(ROWS, STEPS, kv_heads, HD), 2, 0)
    mixed = lax.map(lambda items: attend_head(items[0], items[1], items[2], items[3], items[4], lengths), (query, keys_old, values_old, keys_new, values_new))
    attention = jnp.moveaxis(mixed, 0, 2).reshape(TOKENS, D).astype(jnp.bfloat16)
    results = jnp.stack([input_grad, attention])
    return (results, new_master, new_first, new_second)
```

```python
import math

import jax
import jax.numpy as jnp
from jax import lax
from jax.experimental import pallas as pl
from jax.experimental.pallas import tpu as pltpu
from jax.sharding import PartitionSpec as P

D = 8192
HD = 128
STEPS = 2
OPT_STEP = 100

first_decay = 0.9
second_decay = 0.95
learn_rate = 0.15
weight_decay = 0.1
small_term = 1e-08

N_TP = 8
N_FSDP = 16
SPAN = 16
MASKED = -1e30
OFFSETS = (0, -1, 1, -2, 2, -3, 3, 4)
SAME_CORE = [list(range(0, N_FSDP, 2)), list(range(1, N_FSDP, 2))]


def sibling(block, group):
    pairs = [(group * N_FSDP + f, group * N_FSDP + (f ^ 1)) for f in range(N_FSDP)]
    return lax.ppermute(block, ("group", "fsdp"), pairs)


def along_z(block, group, step):
    pairs = [(group * N_TP + z, group * N_TP + (z + step) % N_TP) for z in range(N_TP)]
    return lax.ppermute(block, ("group", "tp"), pairs)


def final_kernel(place, *refs):
    count = N_TP + 1
    hids, refs = refs[:count], refs[count:]
    w, w_other, queries, cache, reach_of = refs[:5]
    cots, refs = refs[5 : 5 + N_TP], refs[5 + N_TP :]
    cot_other, old, out = refs[:3]
    (
        hid_v, w_v, q_v, c_v, fresh_v, out_v, limit_v, cot_v, old_v,
        hid_sem, w_sem, q_sem, c_sem, out_sem, cot_sem, old_sem,
    ) = refs[3:]
    tokens, features = q_v.shape
    half = tokens // 2
    heads = features // HD
    per = 8

    @pl.when(place[0] == 0)
    def _():
        z, core = place[1], place[2]
        loads = [pltpu.make_async_copy(old, old_v, old_sem)]
        for r in range(N_TP):
            loads.append(
                pltpu.make_async_copy(
                    cots[r].at[:, pl.ds(0, tokens)], cot_v.at[r, pl.ds(0, HD)], cot_sem.at[r]
                )
            )
        loads.append(
            pltpu.make_async_copy(cot_other, cot_v.at[:, pl.ds(HD, HD)], cot_sem.at[N_TP])
        )
        for load in loads:
            load.start()
        for load in loads:
            load.wait()
        stores = []
        for first in range(0, tokens, 128):
            at = slice(first, first + 128)
            total = None
            for r, offset in enumerate(OFFSETS):
                plane = lax.rem(z + (offset + N_TP), N_TP)
                rows = jnp.concatenate(
                    [old_v[2 * plane + core], old_v[2 * plane + 1 - core]], axis=0
                )
                part = lax.dot_general(
                    cot_v[r, :, at],
                    rows,
                    (((0,), (0,)), ((), ())),
                    preferred_element_type=jnp.float32,
                )
                total = part if total is None else total + part
            out_v[at] = (total * (1.0 / math.sqrt(D))).astype(jnp.bfloat16)
            rows = pl.ds(first, 128)
            store = pltpu.make_async_copy(out_v.at[rows], out.at[rows], out_sem.at[first // 128])
            store.start()
            stores.append(store)
        for store in stores:
            store.wait()

    @pl.when(place[0] != 0)
    def _():
        z, core = place[1], place[2]
        loads = [
            pltpu.make_async_copy(v, w_v.at[i], w_sem.at[i]) for i, v in enumerate((w, w_other))
        ]
        for r in range(N_TP - 1):
            loads.append(pltpu.make_async_copy(hids[r], hid_v.at[r], hid_sem.at[r]))
        for i in range(2):
            r = N_TP - 1 + i
            rows = hid_v.at[N_TP - 1, pl.ds(i * half, half)]
            loads.append(pltpu.make_async_copy(hids[r], rows, hid_sem.at[r]))
        loads.append(pltpu.make_async_copy(queries, q_v, q_sem))
        loads.append(pltpu.make_async_copy(cache, c_v, c_sem))
        for load in loads:
            load.start()

        loads[0].wait()
        loads[1].wait()
        total = None
        for r, offset in enumerate(OFFSETS):
            loads[2 + r].wait()
            if r == N_TP - 1:
                loads[3 + r].wait()
            plane = lax.rem(z + (offset + N_TP), N_TP)
            rows = [w_v[i, q, plane] for i in range(2) for q in range(N_TP)]
            part = lax.dot_general(
                hid_v[r],
                jnp.concatenate(rows, axis=0),
                (((1,), (1,)), ((), ())),
                preferred_element_type=jnp.float32,
            )
            total = part if total is None else total + part
        total = total * (1.0 / math.sqrt(D))
        for i in range(2):
            own = total[:, i * 64 : (i + 1) * 64]
            other = total[:, HD + i * 64 : HD + (i + 1) * 64]
            fresh_v[i] = jnp.where(
                core == 0,
                jnp.concatenate([own, other], axis=1),
                jnp.concatenate([other, own], axis=1),
            ).astype(jnp.bfloat16)
        loads[-2].wait()
        loads[-1].wait()

        width = 128 + SPAN
        root = 1.0 / math.sqrt(HD)
        key_at = lax.broadcasted_iota(jnp.int32, (width, heads * SPAN), 0)
        token = lax.broadcasted_iota(jnp.int32, (width, heads * SPAN), 1) % SPAN
        new = key_at - 128
        owner = jnp.where(key_at < 128, key_at // 16, new // STEPS)
        limit = jnp.where(key_at < 128, key_at % 16, 0)
        limit = jnp.where(owner == token // STEPS, jnp.where(new <= token, limit, 99), 99)
        limit_v[...] = limit.astype(jnp.float32)

        stores = []
        for first in range(0, tokens // SPAN, per):
            ids = range(first, first + per)
            scores = []
            for i in ids:
                at = slice(i * SPAN, (i + 1) * SPAN)
                query = jnp.concatenate(
                    [q_v[at, h * HD : (h + 1) * HD] for h in range(heads)], axis=0
                )
                keys = c_v[i * 8 : (i + 1) * 8, 0].reshape(128, HD)
                keys = jnp.concatenate([keys, fresh_v[0, at]], axis=0)
                scores.append(
                    lax.dot_general(
                        keys, query, (((1,), (1,)), ((), ())), preferred_element_type=jnp.float32
                    )
                )
            probs = []
            for i, score in zip(ids, scores):
                seen = limit_v[...] < reach_of[i : i + 1, :]
                score = jnp.where(seen, score * root, MASKED)
                score = jnp.exp(score - jnp.max(score, axis=0, keepdims=True))
                inverse = 1.0 / jnp.sum(score, axis=0, keepdims=True)
                probs.append((score * inverse).astype(jnp.bfloat16))
            for i, prob in zip(ids, probs):
                at = slice(i * SPAN, (i + 1) * SPAN)
                values = c_v[i * 8 : (i + 1) * 8, 1].reshape(128, HD)
                values = jnp.concatenate([values, fresh_v[1, at]], axis=0)
                mixed = lax.dot_general(
                    prob, values, (((0,), (0,)), ((), ())), preferred_element_type=jnp.float32
                ).astype(jnp.bfloat16)
                for h in range(heads):
                    out_v[at, h * HD : (h + 1) * HD] = mixed[h * SPAN : (h + 1) * SPAN]
            rows = pl.ds(first * SPAN, per * SPAN)
            store = pltpu.make_async_copy(out_v.at[rows], out.at[rows], out_sem.at[first // per])
            store.start()
            stores.append(store)
        for store in stores:
            store.wait()


def final(place, hids, w, w_other, queries, cache, lengths, cots, cot_other, old):
    rows = cache.shape[0]
    tokens, features = queries.shape
    reach_of = jnp.repeat(lengths.astype(jnp.float32).reshape(rows // 8, 8), STEPS, axis=1)
    reach_of = jnp.tile(reach_of, (1, features // HD))
    anywhere = pl.BlockSpec(memory_space=pl.ANY)
    in_specs = [pl.BlockSpec(memory_space=pltpu.SMEM)] + [anywhere] * (len(hids) + 4)
    in_specs += [pl.BlockSpec(memory_space=pltpu.VMEM)] + [anywhere] * (len(cots) + 2)
    return pl.pallas_call(
        final_kernel,
        in_specs=in_specs,
        out_specs=anywhere,
        out_shape=jax.ShapeDtypeStruct((tokens, features), jnp.bfloat16),
        scratch_shapes=[
            pltpu.VMEM((N_TP, tokens, features), jnp.bfloat16),
            pltpu.VMEM((2,) + w.shape, jnp.bfloat16),
            pltpu.VMEM((tokens, features), jnp.bfloat16),
            pltpu.VMEM(cache.shape, jnp.bfloat16),
            pltpu.VMEM((2, tokens, HD), jnp.bfloat16),
            pltpu.VMEM((tokens, features), jnp.bfloat16),
            pltpu.VMEM((128 + SPAN, 128), jnp.float32),
            pltpu.VMEM((N_TP, 2 * HD, tokens), jnp.bfloat16),
            pltpu.VMEM(old.shape, jnp.bfloat16),
            pltpu.SemaphoreType.DMA((N_TP + 1,)),
            pltpu.SemaphoreType.DMA((2,)),
            pltpu.SemaphoreType.DMA,
            pltpu.SemaphoreType.DMA,
            pltpu.SemaphoreType.DMA((6,)),
            pltpu.SemaphoreType.DMA((N_TP + 1,)),
            pltpu.SemaphoreType.DMA,
        ],
        compiler_params=pltpu.CompilerParams(vmem_limit_bytes=40 * 1024 * 1024),
        cost_estimate=pl.CostEstimate(
            flops=2 * tokens * D * 2 * HD, bytes_accessed=24 * 2**20, transcendentals=0
        ),
    )(place, *hids, w, w_other, queries, cache, reach_of, *cots, cot_other, old)


def after(block, *others):
    return lax.optimization_barrier((block, *others))[0]


def on_device(hidden, cotangent, queries, kv_cache, lengths, master, moment1, moment2):
    half_index = lax.axis_index("group")
    z = lax.axis_index("tp")
    f = lax.axis_index("fsdp")
    core = f % 2
    rows_in = hidden[0]
    tokens, features = rows_in.shape
    half = tokens // 2
    scale = 1.0 / math.sqrt(D)

    def placed(buffer, block, index):
        return lax.dynamic_update_slice(buffer, block[None], (index % N_TP, 0, 0))

    cot = jnp.transpose(cotangent, (1, 2, 0))
    own = lax.dynamic_slice_in_dim(cot, core * 64, 64, 1)
    other = lax.dynamic_slice_in_dim(cot, (1 - core) * 64, 64, 1)
    cot = jnp.concatenate([own, sibling(other, 0)], axis=2).reshape(128, 2 * tokens)
    own_hidden = after(rows_in, cot[:1, :1])
    hid_chip = jnp.concatenate([rows_in, sibling(own_hidden, 0)], axis=0)

    def products(block):
        product = jnp.dot(block, hid_chip, preferred_element_type=jnp.float32)
        return product.astype(jnp.bfloat16)

    cots = [cot]
    up = down = cot
    hids = [rows_in]
    h_up = along_z(own_hidden, 1, 1)
    h_down = along_z(own_hidden, 1, -1)
    sums = [(products(cot), z)]
    for s in range(1, 4):
        up = along_z(up, 0, 1)
        down = along_z(down, 0, -1)
        if s > 1:
            up, down = after(up, sums[-1][0]), after(down, sums[-1][0])
        if s == 2:
            up, down, h_up, h_down = lax.optimization_barrier((up, down, h_up, h_down))
            hids += [h_up, h_down]
            h_up = along_z(h_up, 1, 1)
            h_down = along_z(h_down, 1, -1)
        cots += [up, down]
        pair = products(jnp.concatenate([up, down], axis=0))
        sums += [(pair[:128], z - s), (pair[128:], z + s)]
    up, down, _ = lax.optimization_barrier((up, down, sums[-1][0]))
    up, down = along_z(up[:64], 0, 1), along_z(down[64:], 0, -1)
    up, down, h_up, h_down = lax.optimization_barrier((up, down, h_up, h_down))
    hids += [h_up, h_down]
    h_up = along_z(h_up, 1, 1)
    h_down = along_z(h_down, 1, -1)
    last = jnp.concatenate([up, down], axis=0)
    cots.append(last)
    sums.append((products(last), z + 4))

    partial = jnp.zeros((N_TP, 128, features), jnp.bfloat16)
    for block, index in sums:
        partial = placed(partial, block, index)
    gathered = lax.all_to_all(partial, "fsdp", 0, 0, axis_index_groups=SAME_CORE)
    cot_other = jnp.stack([block[:, tokens:] for block in cots])
    gathered, cot_other = lax.optimization_barrier((gathered, cot_other))

    gradient = jnp.sum(gathered.astype(jnp.float32), axis=0) * scale
    gradient = jnp.transpose(gradient.reshape(2, 64, features), (1, 0, 2))

    def updated(gradient):
        new_first = first_decay * moment1 + (1.0 - first_decay) * gradient
        new_second = second_decay * moment2 + (1.0 - second_decay) * gradient * gradient
        first_hat = new_first / (1.0 - first_decay**OPT_STEP)
        second_hat = new_second / (1.0 - second_decay**OPT_STEP)
        new_master = master - learn_rate * (
            first_hat / (jnp.sqrt(second_hat) + small_term) + weight_decay * master
        )
        return new_master, new_first, new_second

    serving = jnp.transpose(updated(gradient)[0], (1, 0, 2)).astype(jnp.bfloat16)
    serving = serving.reshape(N_TP, 16, features)

    pieces = lax.all_to_all(serving, "fsdp", 0, 0, axis_index_groups=SAME_CORE)
    pieces = lax.all_to_all(pieces, "tp", 0, 0)
    h_up, h_down, pieces = lax.optimization_barrier((h_up, h_down, pieces))
    hids += [h_up, h_down]
    h_up = along_z(h_up[:half], 1, 1)
    h_down = along_z(h_down[half:], 1, -1)
    hids += [h_up, h_down]
    gradient_late = after(gradient, pieces)
    pieces = lax.ppermute(pieces, "group", [(0, 1)])
    mirrored = lax.ppermute(gradient_late, "group", [(0, 1)])
    cot_other = after(cot_other, pieces)
    w = lax.all_to_all(
        jnp.broadcast_to(pieces[None], (8,) + pieces.shape),
        "fsdp",
        0,
        0,
        axis_index_groups=SAME_CORE,
    )
    cot_other = sibling(cot_other, 0)

    gradient = jnp.where(half_index == 0, gradient, mirrored)
    new_master, new_first, new_second = updated(gradient)
    w, new_master, new_first, new_second, *last_hids = lax.optimization_barrier(
        (w, new_master, new_first, new_second, *hids[-2:])
    )
    hids[-2:] = last_hids
    w_other = lax.ppermute(w, "fsdp", [(i, i ^ 1) for i in range(N_FSDP)])

    old = jnp.transpose(master, (1, 0, 2)).astype(jnp.bfloat16).reshape(128, features)
    old = lax.all_gather(old, "fsdp", axis=0)
    place = jnp.stack([half_index, z, core]).astype(jnp.int32)
    block = final(place, hids, w, w_other, queries, kv_cache, lengths, cots, cot_other, old)
    return (block[None], new_master, new_first, new_second)


def solution(mesh):
    in_specs = (
        P("group", "fsdp", "tp"),
        P("fsdp", None, "tp"),
        P("fsdp", "tp"),
        P("fsdp", None, None, "tp"),
        P("fsdp"),
        P("fsdp", None, "tp"),
        P("fsdp", None, "tp"),
        P("fsdp", None, "tp"),
    )
    out_specs = (
        P("group", "fsdp", "tp"),
        P("fsdp", None, "tp"),
        P("fsdp", None, "tp"),
        P("fsdp", None, "tp"),
    )
    return jax.shard_map(
        on_device, mesh=mesh, in_specs=in_specs, out_specs=out_specs, check_vma=False
    )
```

```python
import functools
import math

import jax
import jax.numpy as jnp
from jax import lax
from jax.experimental import pallas as pl
from jax.experimental.pallas import tpu as pltpu
from jax.sharding import PartitionSpec as P

D = 8192
HD = 128
STEPS = 2
OPT_STEP = 100

first_decay = 0.9
second_decay = 0.95
learn_rate = 0.15
weight_decay = 0.1
small_term = 1e-08

N_TP = 8
N_FSDP = 16
SPAN = 16
MASKED = -1e30
OFFSETS = (0, -1, 1, -2, 2, -3, 3, 4)
HID_PARTS = (
    (0, None), (1, None), (2, None), (3, None), (4, None),
    (5, None), (6, None), (7, 0), (7, 1),
)
SAME_CORE = [list(range(0, N_FSDP, 2)), list(range(1, N_FSDP, 2))]


def sibling(block, group):
    pairs = [(group * N_FSDP + f, group * N_FSDP + (f ^ 1)) for f in range(N_FSDP)]
    return lax.ppermute(block, ("group", "fsdp"), pairs)


def along_z(block, group, step):
    pairs = [(group * N_TP + z, group * N_TP + (z + step) % N_TP) for z in range(N_TP)]
    return lax.ppermute(block, ("group", "tp"), pairs)


def final_kernel(place, *refs):
    count = N_TP + 1
    hids, refs = refs[: len(HID_PARTS)], refs[len(HID_PARTS) :]
    w, w_other, queries, cache, reach_of = refs[:5]
    cots, refs = refs[5 : 5 + count], refs[5 + count :]
    cot_other, old, out = refs[:3]
    (
        hid_v, w_v, q_v, c_v, fresh_v, out_v, limit_v, cot_v, old_v,
        hid_sem, w_sem, q_sem, c_sem, out_sem, cot_sem, old_sem,
    ) = refs[3:]
    tokens, features = q_v.shape
    half = tokens // 2
    heads = features // HD
    per = 8

    @pl.when(place[0] == 0)
    def _():
        z, core = place[1], place[2]
        loads = [pltpu.make_async_copy(old, old_v, old_sem)]
        for i in range(count):
            if i < N_TP - 1:
                rows = cot_v.at[i, pl.ds(0, HD)]
            else:
                rows = cot_v.at[N_TP - 1, pl.ds((i - N_TP + 1) * 64, 64)]
            loads.append(
                pltpu.make_async_copy(cots[i].at[:, pl.ds(0, tokens)], rows, cot_sem.at[i])
            )
        loads.append(
            pltpu.make_async_copy(cot_other, cot_v.at[:, pl.ds(HD, HD)], cot_sem.at[count])
        )
        for load in loads:
            load.start()
        for load in loads:
            load.wait()
        stores = []
        for first in range(0, tokens, 128):
            at = slice(first, first + 128)
            total = None
            for r, offset in enumerate(OFFSETS):
                plane = lax.rem(z + (offset + N_TP), N_TP)
                rows = jnp.concatenate(
                    [old_v[2 * plane + core], old_v[2 * plane + 1 - core]], axis=0
                )
                part = lax.dot_general(
                    cot_v[r, :, at],
                    rows,
                    (((0,), (0,)), ((), ())),
                    preferred_element_type=jnp.float32,
                )
                total = part if total is None else total + part
            out_v[at] = (total * (1.0 / math.sqrt(D))).astype(jnp.bfloat16)
            rows = pl.ds(first, 128)
            store = pltpu.make_async_copy(out_v.at[rows], out.at[rows], out_sem.at[first // 128])
            store.start()
            stores.append(store)
        for store in stores:
            store.wait()

    @pl.when(place[0] != 0)
    def _():
        z, core = place[1], place[2]
        loads = [
            pltpu.make_async_copy(v, w_v.at[i], w_sem.at[i]) for i, v in enumerate((w, w_other))
        ]
        for i, (r, part) in enumerate(HID_PARTS):
            to = hid_v.at[r] if part is None else hid_v.at[r, pl.ds(part * half, half)]
            loads.append(pltpu.make_async_copy(hids[i], to, hid_sem.at[i]))
        loads.append(pltpu.make_async_copy(queries, q_v, q_sem))
        loads.append(pltpu.make_async_copy(cache, c_v, c_sem))
        started = 5
        for load in loads[:started]:
            load.start()

        total = None
        arrived = -1
        for r, offset in enumerate(OFFSETS):
            needed = 1 + max(i for i, v in enumerate(HID_PARTS, 1) if v[0] == r)
            while arrived < needed:
                arrived += 1
                loads[arrived].wait()
                if started < len(loads):
                    loads[started].start()
                    started += 1
            plane = lax.rem(z + (offset + N_TP), N_TP)
            flipped = lax.rem(plane + 4, N_TP)
            rows = [
                v for i in range(2) for v in (w_v[i, plane, :64], w_v[i, flipped, 64:])
            ]
            part = lax.dot_general(
                hid_v[r],
                jnp.concatenate(rows, axis=0),
                (((1,), (1,)), ((), ())),
                preferred_element_type=jnp.float32,
            )
            total = part if total is None else total + part
        total = total * (1.0 / math.sqrt(D))
        for i in range(2):
            own = total[:, i * 64 : (i + 1) * 64]
            other = total[:, HD + i * 64 : HD + (i + 1) * 64]
            fresh_v[i] = jnp.where(
                core == 0,
                jnp.concatenate([own, other], axis=1),
                jnp.concatenate([other, own], axis=1),
            ).astype(jnp.bfloat16)
        loads[-2].wait()
        loads[-1].wait()

        width = 128 + SPAN
        root = 1.0 / math.sqrt(HD)
        key_at = lax.broadcasted_iota(jnp.int32, (width, heads * SPAN), 0)
        token = lax.broadcasted_iota(jnp.int32, (width, heads * SPAN), 1) % SPAN
        new = key_at - 128
        owner = jnp.where(key_at < 128, key_at // 16, new // STEPS)
        limit = jnp.where(key_at < 128, key_at % 16, 0)
        limit = jnp.where(owner == token // STEPS, jnp.where(new <= token, limit, 99), 99)
        limit_v[...] = limit.astype(jnp.float32)

        stores = []
        for first in range(0, tokens // SPAN, per):
            ids = range(first, first + per)
            scores = []
            for i in ids:
                at = slice(i * SPAN, (i + 1) * SPAN)
                query = jnp.concatenate(
                    [q_v[at, h * HD : (h + 1) * HD] for h in range(heads)], axis=0
                )
                keys = c_v[i * 8 : (i + 1) * 8, 0].reshape(128, HD)
                keys = jnp.concatenate([keys, fresh_v[0, at]], axis=0)
                scores.append(
                    lax.dot_general(
                        keys, query, (((1,), (1,)), ((), ())), preferred_element_type=jnp.float32
                    )
                )
            probs = []
            for i, score in zip(ids, scores):
                seen = limit_v[...] < reach_of[i : i + 1, :]
                score = jnp.where(seen, score * root, MASKED)
                score = jnp.exp(score - jnp.max(score, axis=0, keepdims=True))
                inverse = 1.0 / jnp.sum(score, axis=0, keepdims=True)
                probs.append((score * inverse).astype(jnp.bfloat16))
            for i, prob in zip(ids, probs):
                at = slice(i * SPAN, (i + 1) * SPAN)
                values = c_v[i * 8 : (i + 1) * 8, 1].reshape(128, HD)
                values = jnp.concatenate([values, fresh_v[1, at]], axis=0)
                mixed = lax.dot_general(
                    prob, values, (((0,), (0,)), ((), ())), preferred_element_type=jnp.float32
                ).astype(jnp.bfloat16)
                for h in range(heads):
                    out_v[at, h * HD : (h + 1) * HD] = mixed[h * SPAN : (h + 1) * SPAN]
            rows = pl.ds(first * SPAN, per * SPAN)
            store = pltpu.make_async_copy(out_v.at[rows], out.at[rows], out_sem.at[first // per])
            store.start()
            stores.append(store)
        for store in stores:
            store.wait()


def final(place, hids, w, w_other, queries, cache, reach_of, cots, cot_other, old):
    tokens, features = queries.shape
    anywhere = pl.BlockSpec(memory_space=pl.ANY)
    in_specs = [pl.BlockSpec(memory_space=pltpu.SMEM)] + [anywhere] * (len(hids) + 4)
    in_specs += [pl.BlockSpec(memory_space=pltpu.VMEM)] + [anywhere] * (len(cots) + 2)
    return pl.pallas_call(
        final_kernel,
        in_specs=in_specs,
        out_specs=anywhere,
        out_shape=jax.ShapeDtypeStruct((tokens, features), jnp.bfloat16),
        scratch_shapes=[
            pltpu.VMEM((N_TP, tokens, features), jnp.bfloat16),
            pltpu.VMEM((2,) + w.shape, jnp.bfloat16),
            pltpu.VMEM((tokens, features), jnp.bfloat16),
            pltpu.VMEM(cache.shape, jnp.bfloat16),
            pltpu.VMEM((2, tokens, HD), jnp.bfloat16),
            pltpu.VMEM((tokens, features), jnp.bfloat16),
            pltpu.VMEM((128 + SPAN, 128), jnp.float32),
            pltpu.VMEM((N_TP, 2 * HD, tokens), jnp.bfloat16),
            pltpu.VMEM(old.shape, jnp.bfloat16),
            pltpu.SemaphoreType.DMA((len(HID_PARTS),)),
            pltpu.SemaphoreType.DMA((2,)),
            pltpu.SemaphoreType.DMA,
            pltpu.SemaphoreType.DMA,
            pltpu.SemaphoreType.DMA((6,)),
            pltpu.SemaphoreType.DMA((N_TP + 2,)),
            pltpu.SemaphoreType.DMA,
        ],
        compiler_params=pltpu.CompilerParams(vmem_limit_bytes=56 * 1024 * 1024),
        cost_estimate=pl.CostEstimate(
            flops=2 * tokens * D * 2 * HD, bytes_accessed=24 * 2**20, transcendentals=0
        ),
    )(place, *hids, w, w_other, queries, cache, reach_of, *cots, cot_other, old)


def split_kernel(place, cot, own, other, turned):
    @pl.when(place[0] == 0)
    def _():
        core = place[2]
        for g in range(2):
            turned[...] = cot[:, g * HD : (g + 1) * HD].T
            rows = slice(g * 64, (g + 1) * 64)
            own[rows] = turned[pl.ds(pl.multiple_of(core * 64, 64), 64)]
            other[rows] = turned[pl.ds(pl.multiple_of((1 - core) * 64, 64), 64)]


def split(place, cot):
    turned = jax.ShapeDtypeStruct((HD, cot.shape[0]), cot.dtype)
    return pl.pallas_call(
        split_kernel,
        in_specs=[
            pl.BlockSpec(memory_space=pltpu.SMEM),
            pl.BlockSpec(memory_space=pltpu.VMEM),
        ],
        out_specs=[pl.BlockSpec(memory_space=pltpu.VMEM)] * 2,
        out_shape=[turned, turned],
        scratch_shapes=[pltpu.VMEM(turned.shape, turned.dtype)],
        compiler_params=pltpu.CompilerParams(vmem_limit_bytes=8 * 1024 * 1024),
    )(place, cot)


def product_kernel(place, *refs, ids, halves, first):
    count = len(ids)
    blocks, refs = refs[: count * halves], refs[count * halves :]
    hid_own, hid_other = refs[:2]
    refs = refs[2:] if first else refs[4:]
    partial, cot_other, block_v, hid_v, out_v, block_sem, hid_sem, out_sem, cot_sem = refs
    tokens, features = hid_own.shape
    rows = HD // halves

    @pl.when(place[0] == 0)
    def _():
        z = place[1]
        loads = [
            pltpu.make_async_copy(v, hid_v.at[pl.ds(i * tokens, tokens)], hid_sem.at[i])
            for i, v in enumerate((hid_own, hid_other))
        ]
        stores = []
        for i, block in enumerate(blocks):
            at = pl.ds(i * rows, rows)
            loads.append(pltpu.make_async_copy(block, block_v.at[at], block_sem.at[i]))
            part = cot_other.at[ids[i // halves], pl.ds(i % halves * rows, rows)]
            stores.append(
                pltpu.make_async_copy(block.at[:, pl.ds(tokens, tokens)], part, cot_sem.at[i])
            )
        for copy in loads + stores:
            copy.start()
        for load in loads:
            load.wait()
        for n in range(0, features, 256):
            part = jnp.dot(
                block_v[...], hid_v[:, n : n + 256], preferred_element_type=jnp.float32
            )
            out_v[:, n : n + 256] = part.astype(jnp.bfloat16)
        for i, r in enumerate(ids):
            plane = lax.rem(z + (OFFSETS[r] + N_TP), N_TP)
            store = pltpu.make_async_copy(
                out_v.at[pl.ds(i * HD, HD)], partial.at[plane], out_sem.at[i]
            )
            store.start()
            stores.append(store)
        for store in stores:
            store.wait()


def product(place, ids, blocks, hid_own, hid_other, before=()):
    first = not before
    tokens, features = hid_own.shape
    operands = (place, *blocks, hid_own, hid_other, *before)
    rows = len(ids) * HD
    return pl.pallas_call(
        functools.partial(
            product_kernel, ids=ids, halves=len(blocks) // len(ids), first=first
        ),
        in_specs=[pl.BlockSpec(memory_space=pltpu.SMEM)]
        + [pl.BlockSpec(memory_space=pl.ANY)] * (len(operands) - 1),
        out_specs=[pl.BlockSpec(memory_space=pl.ANY)] * 2,
        out_shape=[
            jax.ShapeDtypeStruct((N_TP, HD, features), jnp.bfloat16),
            jax.ShapeDtypeStruct((N_TP, HD, tokens), jnp.bfloat16),
        ],
        input_output_aliases={} if first else {len(operands) - 2: 0, len(operands) - 1: 1},
        scratch_shapes=[
            pltpu.VMEM((rows, 2 * tokens), jnp.bfloat16),
            pltpu.VMEM((2 * tokens, features), jnp.bfloat16),
            pltpu.VMEM((rows, features), jnp.bfloat16),
            pltpu.SemaphoreType.DMA((len(blocks),)),
            pltpu.SemaphoreType.DMA((2,)),
            pltpu.SemaphoreType.DMA((len(ids),)),
            pltpu.SemaphoreType.DMA((len(blocks),)),
        ],
        compiler_params=pltpu.CompilerParams(vmem_limit_bytes=16 * 1024 * 1024),
        cost_estimate=pl.CostEstimate(
            flops=4 * rows * tokens * features, bytes_accessed=12 * 2**20, transcendentals=0
        ),
    )(*operands)


def adam(gradient, master, moment1, moment2):
    new_first = first_decay * moment1 + (1.0 - first_decay) * gradient
    new_second = second_decay * moment2 + (1.0 - second_decay) * gradient * gradient
    first_hat = new_first / (1.0 - first_decay**OPT_STEP)
    second_hat = new_second / (1.0 - second_decay**OPT_STEP)
    new_master = master - learn_rate * (
        first_hat / (jnp.sqrt(second_hat) + small_term) + weight_decay * master
    )
    return new_master, new_first, new_second


def adam_kernel(place, gradient, mirrored, master, moment1, moment2, *outs):
    chosen = jnp.where(place[0] == 0, gradient[...], mirrored[...])
    for out, value in zip(outs, adam(chosen, master[...], moment1[...], moment2[...])):
        out[...] = value


def adam_outputs(place, *arrays):
    return pl.pallas_call(
        adam_kernel,
        in_specs=[pl.BlockSpec(memory_space=pltpu.SMEM)]
        + [pl.BlockSpec(memory_space=pltpu.VMEM)] * 5,
        out_specs=[pl.BlockSpec(memory_space=pltpu.VMEM)] * 3,
        out_shape=[jax.ShapeDtypeStruct(arrays[0].shape, jnp.float32)] * 3,
        compiler_params=pltpu.CompilerParams(vmem_limit_bytes=16 * 1024 * 1024),
    )(place, *arrays)


def after(block, *others):
    return lax.optimization_barrier((block, *others))[0]


def on_device(hidden, cotangent, queries, kv_cache, lengths, master, moment1, moment2):
    half_index = lax.axis_index("group")
    z = lax.axis_index("tp")
    f = lax.axis_index("fsdp")
    core = f % 2
    rows_in = hidden[0]
    tokens, features = rows_in.shape
    half = tokens // 2
    scale = 1.0 / math.sqrt(D)

    place = jnp.stack([half_index, z, core]).astype(jnp.int32)

    own, other = split(place, cotangent.reshape(tokens, 2 * HD))
    cot = jnp.concatenate([own, sibling(other, 0)], axis=1)

    cots = [cot]
    own_hidden = after(rows_in, cot)
    hids = [rows_in]
    h_up, h_down = along_z(own_hidden, 1, 1), along_z(own_hidden, 1, -1)
    up, down = along_z(cot, 0, 1), along_z(cot, 0, -1)
    cots += [up, down]
    hid_other = sibling(after(rows_in, up, down), 0)
    up, down = along_z(up, 0, 1), along_z(down, 0, -1)
    cots += [up, down]
    up, down = after(up, h_up, h_down), after(down, h_up, h_down)
    hids += [h_up, h_down]
    h_up, h_down = along_z(h_up, 1, 1), along_z(h_down, 1, -1)
    up, down = along_z(up, 0, 1), along_z(down, 0, -1)
    cots += [up, down]
    sums = product(place, (0, 1, 2, 3, 4), cots[:5], rows_in, hid_other)
    up, down = after(up, sums[0]), after(down, sums[0])
    up, down = along_z(up[:64], 0, 1), along_z(down[64:], 0, -1)
    sums = product(place, (5, 6), cots[5:], rows_in, hid_other, sums)
    old = jnp.transpose(master, (1, 0, 2)).astype(jnp.bfloat16).reshape(128, features)
    old = lax.all_gather(old, "fsdp", axis=0)
    sums = (after(sums[0], up, down, old), sums[1])
    partial, cot_other = product(place, (7,), (up, down), rows_in, hid_other, sums)
    cots += [up, down]
    gathered = lax.all_to_all(partial, "fsdp", 0, 0, axis_index_groups=SAME_CORE)
    gathered, h_up, h_down = lax.optimization_barrier((gathered, h_up, h_down))
    hids += [h_up, h_down]
    h_up, h_down = along_z(h_up, 1, 1), along_z(h_down, 1, -1)
    gradient = jnp.sum(gathered.astype(jnp.float32), axis=0) * scale
    gradient = jnp.transpose(gradient.reshape(2, 64, features), (1, 0, 2))

    serving = jnp.transpose(adam(gradient, master, moment1, moment2)[0], (1, 0, 2)).astype(jnp.bfloat16)
    serving = serving.reshape(128, features)

    def across(rows, flip):
        pairs = [
            ((p * 2 + c) * N_TP + plane, (N_FSDP + (plane ^ flip) * 2 + c) * N_TP + p)
            for p in range(8)
            for c in range(2)
            for plane in range(N_TP)
        ]
        return lax.ppermute(rows, ("group", "fsdp", "tp"), pairs)

    keys, values = across(serving[:64], 0), across(serving[64:], 4)
    hids += [h_up, h_down]
    far_first, far_second = along_z(h_up[:half], 1, 1), along_z(h_down[half:], 1, -1)
    hids += [far_first, far_second]
    cot_other = after(cot_other, keys)
    pieces = jnp.concatenate([keys, values], axis=0)
    w = lax.all_to_all(
        jnp.broadcast_to(pieces[None], (8,) + pieces.shape),
        "fsdp",
        0,
        0,
        axis_index_groups=SAME_CORE,
    )
    cot_other = sibling(cot_other, 0)
    reach_of = jnp.repeat(lengths.astype(jnp.float32).reshape(-1, 8), STEPS, axis=1)
    reach_of = jnp.tile(reach_of, (1, queries.shape[1] // HD))
    w, reach_of, gradient, far_first, far_second = lax.optimization_barrier(
        (w, reach_of, gradient, far_first, far_second)
    )
    hids[-2:] = [far_first, far_second]
    mirrored = lax.ppermute(gradient, "group", [(0, 1)])
    w_other = lax.ppermute(w, "fsdp", [(i, i ^ 1) for i in range(N_FSDP)])
    block = final(place, hids, w, w_other, queries, kv_cache, reach_of, cots, cot_other, old)
    mirrored, block = lax.optimization_barrier((mirrored, block))
    outs = adam_outputs(place, gradient, mirrored, master, moment1, moment2)
    return (block[None], *outs)


def solution(mesh):
    in_specs = (
        P("group", "fsdp", "tp"),
        P("fsdp", None, "tp"),
        P("fsdp", "tp"),
        P("fsdp", None, None, "tp"),
        P("fsdp"),
        P("fsdp", None, "tp"),
        P("fsdp", None, "tp"),
        P("fsdp", None, "tp"),
    )
    out_specs = (
        P("group", "fsdp", "tp"),
        P("fsdp", None, "tp"),
        P("fsdp", None, "tp"),
        P("fsdp", None, "tp"),
    )
    return jax.shard_map(
        on_device, mesh=mesh, in_specs=in_specs, out_specs=out_specs, check_vma=False
    )
```

```python
import functools
import math

import jax
import jax.numpy as jnp
from jax import lax
from jax.experimental import pallas as pl
from jax.experimental.pallas import tpu as pltpu
from jax.sharding import PartitionSpec as P

D = 8192
HD = 128
STEPS = 2
OPT_STEP = 100

first_decay = 0.9
second_decay = 0.95
learn_rate = 0.15
weight_decay = 0.1
small_term = 1e-08

N_TP = 8
N_FSDP = 16
SPAN = 16
MASKED = -1e30
OFFSETS = (0, -1, 1, -2, 2, -3, 3, 4)
HID_PARTS = (
    (0, None), (1, None), (2, None), (3, None), (4, None),
    (5, None), (6, None), (7, 0), (7, 1),
)
SAME_CORE = [list(range(0, N_FSDP, 2)), list(range(1, N_FSDP, 2))]


def sibling(block, group):
    pairs = [(group * N_FSDP + f, group * N_FSDP + (f ^ 1)) for f in range(N_FSDP)]
    return lax.ppermute(block, ("group", "fsdp"), pairs)


def along_z(block, group, step):
    pairs = [(group * N_TP + z, group * N_TP + (z + step) % N_TP) for z in range(N_TP)]
    return lax.ppermute(block, ("group", "tp"), pairs)


def final_kernel(place, *refs):
    count = N_TP + 1
    hids, refs = refs[: len(HID_PARTS)], refs[len(HID_PARTS) :]
    w, w_other, queries, cache, reach_of = refs[:5]
    cots, refs = refs[5 : 5 + count], refs[5 + count :]
    cot_other, old, out = refs[:3]
    (
        hid_v, w_v, q_v, c_v, fresh_v, out_v, limit_v, cot_v, old_v,
        hid_sem, w_sem, q_sem, c_sem, out_sem, cot_sem, old_sem,
    ) = refs[3:]
    tokens, features = q_v.shape
    half = tokens // 2
    heads = features // HD
    per = 8

    @pl.when(place[0] == 0)
    def _():
        z, core = place[1], place[2]
        loads = [pltpu.make_async_copy(old, old_v, old_sem)]
        for i in range(count):
            if i < N_TP - 1:
                rows = cot_v.at[i, pl.ds(0, HD)]
            else:
                rows = cot_v.at[N_TP - 1, pl.ds((i - N_TP + 1) * 64, 64)]
            loads.append(
                pltpu.make_async_copy(cots[i].at[:, pl.ds(0, tokens)], rows, cot_sem.at[i])
            )
        loads.append(
            pltpu.make_async_copy(cot_other, cot_v.at[:, pl.ds(HD, HD)], cot_sem.at[count])
        )
        for load in loads:
            load.start()
        for load in loads:
            load.wait()
        stores = []
        for first in range(0, tokens, 128):
            at = slice(first, first + 128)
            total = None
            for r, offset in enumerate(OFFSETS):
                plane = lax.rem(z + (offset + N_TP), N_TP)
                rows = jnp.concatenate(
                    [old_v[2 * plane + core], old_v[2 * plane + 1 - core]], axis=0
                )
                part = lax.dot_general(
                    cot_v[r, :, at],
                    rows,
                    (((0,), (0,)), ((), ())),
                    preferred_element_type=jnp.float32,
                )
                total = part if total is None else total + part
            out_v[at] = (total * (1.0 / math.sqrt(D))).astype(jnp.bfloat16)
            rows = pl.ds(first, 128)
            store = pltpu.make_async_copy(out_v.at[rows], out.at[rows], out_sem.at[first // 128])
            store.start()
            stores.append(store)
        for store in stores:
            store.wait()

    @pl.when(place[0] != 0)
    def _():
        z, core = place[1], place[2]
        loads = [
            pltpu.make_async_copy(v, w_v.at[i], w_sem.at[i]) for i, v in enumerate((w, w_other))
        ]
        for i, (r, part) in enumerate(HID_PARTS):
            to = hid_v.at[r] if part is None else hid_v.at[r, pl.ds(part * half, half)]
            loads.append(pltpu.make_async_copy(hids[i], to, hid_sem.at[i]))
        loads.append(pltpu.make_async_copy(queries, q_v, q_sem))
        loads.append(pltpu.make_async_copy(cache, c_v, c_sem))
        started = 5
        for load in loads[:started]:
            load.start()

        total = None
        arrived = -1
        for r, offset in enumerate(OFFSETS):
            needed = 1 + max(i for i, v in enumerate(HID_PARTS, 1) if v[0] == r)
            while arrived < needed:
                arrived += 1
                loads[arrived].wait()
                if started < len(loads):
                    loads[started].start()
                    started += 1
            plane = lax.rem(z + (offset + N_TP), N_TP)
            flipped = lax.rem(plane + 4, N_TP)
            rows = [
                v for i in range(2) for v in (w_v[i, plane, :64], w_v[i, flipped, 64:])
            ]
            part = lax.dot_general(
                hid_v[r],
                jnp.concatenate(rows, axis=0),
                (((1,), (1,)), ((), ())),
                preferred_element_type=jnp.float32,
            )
            total = part if total is None else total + part
        total = total * (1.0 / math.sqrt(D))
        for i in range(2):
            own = total[:, i * 64 : (i + 1) * 64]
            other = total[:, HD + i * 64 : HD + (i + 1) * 64]
            fresh_v[i] = jnp.where(
                core == 0,
                jnp.concatenate([own, other], axis=1),
                jnp.concatenate([other, own], axis=1),
            ).astype(jnp.bfloat16)
        loads[-2].wait()
        loads[-1].wait()

        width = 128 + SPAN
        root = 1.0 / math.sqrt(HD)
        key_at = lax.broadcasted_iota(jnp.int32, (width, heads * SPAN), 0)
        token = lax.broadcasted_iota(jnp.int32, (width, heads * SPAN), 1) % SPAN
        new = key_at - 128
        owner = jnp.where(key_at < 128, key_at // 16, new // STEPS)
        limit = jnp.where(key_at < 128, key_at % 16, 0)
        limit = jnp.where(owner == token // STEPS, jnp.where(new <= token, limit, 99), 99)
        limit_v[...] = limit.astype(jnp.float32)

        stores = []
        for first in range(0, tokens // SPAN, per):
            ids = range(first, first + per)
            scores = []
            for i in ids:
                at = slice(i * SPAN, (i + 1) * SPAN)
                query = jnp.concatenate(
                    [q_v[at, h * HD : (h + 1) * HD] for h in range(heads)], axis=0
                )
                keys = c_v[i * 8 : (i + 1) * 8, 0].reshape(128, HD)
                keys = jnp.concatenate([keys, fresh_v[0, at]], axis=0)
                scores.append(
                    lax.dot_general(
                        keys, query, (((1,), (1,)), ((), ())), preferred_element_type=jnp.float32
                    )
                )
            probs = []
            for i, score in zip(ids, scores):
                seen = limit_v[...] < reach_of[i : i + 1, :]
                score = jnp.where(seen, score * root, MASKED)
                score = jnp.exp(score - jnp.max(score, axis=0, keepdims=True))
                inverse = 1.0 / jnp.sum(score, axis=0, keepdims=True)
                probs.append((score * inverse).astype(jnp.bfloat16))
            for i, prob in zip(ids, probs):
                at = slice(i * SPAN, (i + 1) * SPAN)
                values = c_v[i * 8 : (i + 1) * 8, 1].reshape(128, HD)
                values = jnp.concatenate([values, fresh_v[1, at]], axis=0)
                mixed = lax.dot_general(
                    prob, values, (((0,), (0,)), ((), ())), preferred_element_type=jnp.float32
                ).astype(jnp.bfloat16)
                for h in range(heads):
                    out_v[at, h * HD : (h + 1) * HD] = mixed[h * SPAN : (h + 1) * SPAN]
            rows = pl.ds(first * SPAN, per * SPAN)
            store = pltpu.make_async_copy(out_v.at[rows], out.at[rows], out_sem.at[first // per])
            store.start()
            stores.append(store)
        for store in stores:
            store.wait()


def final(place, hids, w, w_other, queries, cache, reach_of, cots, cot_other, old):
    tokens, features = queries.shape
    anywhere = pl.BlockSpec(memory_space=pl.ANY)
    in_specs = [pl.BlockSpec(memory_space=pltpu.SMEM)] + [anywhere] * (len(hids) + 4)
    in_specs += [pl.BlockSpec(memory_space=pltpu.VMEM)] + [anywhere] * (len(cots) + 2)
    return pl.pallas_call(
        final_kernel,
        in_specs=in_specs,
        out_specs=anywhere,
        out_shape=jax.ShapeDtypeStruct((tokens, features), jnp.bfloat16),
        scratch_shapes=[
            pltpu.VMEM((N_TP, tokens, features), jnp.bfloat16),
            pltpu.VMEM((2,) + w.shape, jnp.bfloat16),
            pltpu.VMEM((tokens, features), jnp.bfloat16),
            pltpu.VMEM(cache.shape, jnp.bfloat16),
            pltpu.VMEM((2, tokens, HD), jnp.bfloat16),
            pltpu.VMEM((tokens, features), jnp.bfloat16),
            pltpu.VMEM((128 + SPAN, 128), jnp.float32),
            pltpu.VMEM((N_TP, 2 * HD, tokens), jnp.bfloat16),
            pltpu.VMEM(old.shape, jnp.bfloat16),
            pltpu.SemaphoreType.DMA((len(HID_PARTS),)),
            pltpu.SemaphoreType.DMA((2,)),
            pltpu.SemaphoreType.DMA,
            pltpu.SemaphoreType.DMA,
            pltpu.SemaphoreType.DMA((6,)),
            pltpu.SemaphoreType.DMA((N_TP + 2,)),
            pltpu.SemaphoreType.DMA,
        ],
        compiler_params=pltpu.CompilerParams(vmem_limit_bytes=56 * 1024 * 1024),
        cost_estimate=pl.CostEstimate(
            flops=2 * tokens * D * 2 * HD, bytes_accessed=24 * 2**20, transcendentals=0
        ),
    )(place, *hids, w, w_other, queries, cache, reach_of, *cots, cot_other, old)


def split_kernel(place, cot, own, other, turned):
    @pl.when(place[0] == 0)
    def _():
        core = place[2]
        for g in range(2):
            turned[...] = cot[:, g * HD : (g + 1) * HD].T
            rows = slice(g * 64, (g + 1) * 64)
            own[rows] = turned[pl.ds(pl.multiple_of(core * 64, 64), 64)]
            other[rows] = turned[pl.ds(pl.multiple_of((1 - core) * 64, 64), 64)]


def split(place, cot):
    turned = jax.ShapeDtypeStruct((HD, cot.shape[0]), cot.dtype)
    return pl.pallas_call(
        split_kernel,
        in_specs=[
            pl.BlockSpec(memory_space=pltpu.SMEM),
            pl.BlockSpec(memory_space=pltpu.VMEM),
        ],
        out_specs=[pl.BlockSpec(memory_space=pltpu.VMEM)] * 2,
        out_shape=[turned, turned],
        scratch_shapes=[pltpu.VMEM(turned.shape, turned.dtype)],
        compiler_params=pltpu.CompilerParams(vmem_limit_bytes=8 * 1024 * 1024),
    )(place, cot)


def product_kernel(place, *refs, ids, halves, first):
    count = len(ids)
    blocks, refs = refs[: count * halves], refs[count * halves :]
    hid_own, hid_other = refs[:2]
    refs = refs[2:] if first else refs[3:]
    partial, cot_other, block_v, hid_v, out_v, block_sem, hid_sem, out_sem, cot_sem = refs
    tokens, features = hid_own.shape
    rows = HD // halves

    @pl.when(place[0] == 0)
    def _():
        z = place[1]
        loads = [
            pltpu.make_async_copy(v, hid_v.at[pl.ds(i * tokens, tokens)], hid_sem.at[i])
            for i, v in enumerate((hid_own, hid_other))
        ]
        stores = []
        for i, block in enumerate(blocks):
            at = pl.ds(i * rows, rows)
            loads.append(pltpu.make_async_copy(block, block_v.at[at], block_sem.at[i]))
            part = cot_other.at[i // halves, pl.ds(i % halves * rows, rows)]
            stores.append(
                pltpu.make_async_copy(block.at[:, pl.ds(tokens, tokens)], part, cot_sem.at[i])
            )
        for copy in loads + stores:
            copy.start()
        for load in loads:
            load.wait()
        for n in range(0, features, 256):
            part = jnp.dot(
                block_v[...], hid_v[:, n : n + 256], preferred_element_type=jnp.float32
            )
            out_v[:, n : n + 256] = part.astype(jnp.bfloat16)
        for i, r in enumerate(ids):
            plane = lax.rem(z + (OFFSETS[r] + N_TP), N_TP)
            store = pltpu.make_async_copy(
                out_v.at[pl.ds(i * HD, HD)], partial.at[plane], out_sem.at[i]
            )
            store.start()
            stores.append(store)
        for store in stores:
            store.wait()


def product(place, ids, blocks, hid_own, hid_other, *before):
    first = not before
    tokens, features = hid_own.shape
    operands = (place, *blocks, hid_own, hid_other, *before)
    rows = len(ids) * HD
    return pl.pallas_call(
        functools.partial(
            product_kernel, ids=ids, halves=len(blocks) // len(ids), first=first
        ),
        in_specs=[pl.BlockSpec(memory_space=pltpu.SMEM)]
        + [pl.BlockSpec(memory_space=pl.ANY)] * (len(operands) - 1),
        out_specs=[pl.BlockSpec(memory_space=pl.ANY)] * 2,
        out_shape=[
            jax.ShapeDtypeStruct((N_TP, HD, features), jnp.bfloat16),
            jax.ShapeDtypeStruct((len(ids), HD, tokens), jnp.bfloat16),
        ],
        input_output_aliases={} if first else {len(operands) - 1: 0},
        scratch_shapes=[
            pltpu.VMEM((rows, 2 * tokens), jnp.bfloat16),
            pltpu.VMEM((2 * tokens, features), jnp.bfloat16),
            pltpu.VMEM((rows, features), jnp.bfloat16),
            pltpu.SemaphoreType.DMA((len(blocks),)),
            pltpu.SemaphoreType.DMA((2,)),
            pltpu.SemaphoreType.DMA((len(ids),)),
            pltpu.SemaphoreType.DMA((len(blocks),)),
        ],
        compiler_params=pltpu.CompilerParams(vmem_limit_bytes=16 * 1024 * 1024),
        cost_estimate=pl.CostEstimate(
            flops=4 * rows * tokens * features, bytes_accessed=12 * 2**20, transcendentals=0
        ),
    )(*operands)


def adam(gradient, master, moment1, moment2):
    new_first = first_decay * moment1 + (1.0 - first_decay) * gradient
    new_second = second_decay * moment2 + (1.0 - second_decay) * gradient * gradient
    first_hat = new_first / (1.0 - first_decay**OPT_STEP)
    second_hat = new_second / (1.0 - second_decay**OPT_STEP)
    new_master = master - learn_rate * (
        first_hat / (jnp.sqrt(second_hat) + small_term) + weight_decay * master
    )
    return new_master, new_first, new_second


def adam_kernel(place, gradient, mirrored, master, moment1, moment2, *outs):
    chosen = jnp.where(place[0] == 0, gradient[...], mirrored[...])
    for out, value in zip(outs, adam(chosen, master[...], moment1[...], moment2[...])):
        out[...] = value


def adam_outputs(place, *arrays):
    return pl.pallas_call(
        adam_kernel,
        in_specs=[pl.BlockSpec(memory_space=pltpu.SMEM)]
        + [pl.BlockSpec(memory_space=pltpu.VMEM)] * 5,
        out_specs=[pl.BlockSpec(memory_space=pltpu.VMEM)] * 3,
        out_shape=[jax.ShapeDtypeStruct(arrays[0].shape, jnp.float32)] * 3,
        compiler_params=pltpu.CompilerParams(vmem_limit_bytes=16 * 1024 * 1024),
    )(place, *arrays)


def after(block, *others):
    return lax.optimization_barrier((block, *others))[0]


def on_device(hidden, cotangent, queries, kv_cache, lengths, master, moment1, moment2):
    half_index = lax.axis_index("group")
    z = lax.axis_index("tp")
    f = lax.axis_index("fsdp")
    core = f % 2
    rows_in = hidden[0]
    tokens, features = rows_in.shape
    half = tokens // 2
    scale = 1.0 / math.sqrt(D)

    place = jnp.stack([half_index, z, core]).astype(jnp.int32)

    own, other = split(place, cotangent.reshape(tokens, 2 * HD))
    cot = jnp.concatenate([own, sibling(other, 0)], axis=1)

    cots = [cot]
    own_hidden = after(rows_in, cot)
    hids = [rows_in]
    h_up, h_down = along_z(own_hidden, 1, 1), along_z(own_hidden, 1, -1)
    up, down = along_z(cot, 0, 1), along_z(cot, 0, -1)
    cots += [up, down]
    hid_other = sibling(after(rows_in, up, down), 0)
    up, down = along_z(up, 0, 1), along_z(down, 0, -1)
    cots += [up, down]
    up, down = after(up, h_up, h_down), after(down, h_up, h_down)
    hids += [h_up, h_down]
    h_up, h_down = along_z(h_up, 1, 1), along_z(h_down, 1, -1)
    far_up, far_down = along_z(up[:64], 0, 2), along_z(down[64:], 0, -2)
    up, down = along_z(up, 0, 1), along_z(down, 0, -1)
    cots += [up, down]
    partial, others = product(place, (0, 1, 2, 3, 4), cots[:5], rows_in, hid_other)
    partial, more = product(place, (5, 6), cots[5:], rows_in, hid_other, partial)
    old = jnp.transpose(master, (1, 0, 2)).astype(jnp.bfloat16).reshape(128, features)
    old = lax.all_gather(old, "fsdp", axis=0)
    partial, up, down, old = lax.optimization_barrier((partial, far_up, far_down, old))
    partial, last = product(place, (7,), (up, down), rows_in, hid_other, partial)
    cots += [up, down]
    gathered = lax.all_to_all(partial, "fsdp", 0, 0, axis_index_groups=SAME_CORE)
    gradient = jnp.sum(gathered.astype(jnp.float32), axis=0) * scale
    gradient = jnp.transpose(gradient.reshape(2, 64, features), (1, 0, 2))

    serving = jnp.transpose(adam(gradient, master, moment1, moment2)[0], (1, 0, 2)).astype(jnp.bfloat16)
    serving = serving.reshape(128, features)
    serving, h_up, h_down = lax.optimization_barrier((serving, h_up, h_down))
    hids += [h_up, h_down]
    h_up, h_down = along_z(h_up, 1, 1), along_z(h_down, 1, -1)

    def across(rows, flip):
        pairs = [
            ((p * 2 + c) * N_TP + plane, (N_FSDP + (plane ^ flip) * 2 + c) * N_TP + p)
            for p in range(8)
            for c in range(2)
            for plane in range(N_TP)
        ]
        return lax.ppermute(rows, ("group", "fsdp", "tp"), pairs)

    keys, values = across(serving[:64], 0), across(serving[64:], 4)
    hids += [h_up, h_down]
    far_first, far_second = along_z(h_up[:half], 1, 1), along_z(h_down[half:], 1, -1)
    hids += [far_first, far_second]
    cot_other = jnp.concatenate([others, more, last], axis=0)
    keys, values, cot_other = lax.optimization_barrier((keys, values, cot_other))
    pieces = jnp.concatenate([keys, values], axis=0)
    w = lax.all_to_all(
        jnp.broadcast_to(pieces[None], (8,) + pieces.shape),
        "fsdp",
        0,
        0,
        axis_index_groups=SAME_CORE,
    )
    cot_other = sibling(cot_other, 0)
    reach_of = jnp.repeat(lengths.astype(jnp.float32).reshape(-1, 8), STEPS, axis=1)
    reach_of = jnp.tile(reach_of, (1, queries.shape[1] // HD))
    w, reach_of, gradient, far_first, far_second, cot_other = lax.optimization_barrier(
        (w, reach_of, gradient, far_first, far_second, cot_other)
    )
    hids[-2:] = [far_first, far_second]
    mirrored = lax.ppermute(gradient, "group", [(0, 1)])
    w_other = lax.ppermute(w, "fsdp", [(i, i ^ 1) for i in range(N_FSDP)])
    block = final(place, hids, w, w_other, queries, kv_cache, reach_of, cots, cot_other, old)
    mirrored, block = lax.optimization_barrier((mirrored, block))
    outs = adam_outputs(place, gradient, mirrored, master, moment1, moment2)
    return (block[None], *outs)


def solution(mesh):
    in_specs = (
        P("group", "fsdp", "tp"),
        P("fsdp", None, "tp"),
        P("fsdp", "tp"),
        P("fsdp", None, None, "tp"),
        P("fsdp"),
        P("fsdp", None, "tp"),
        P("fsdp", None, "tp"),
        P("fsdp", None, "tp"),
    )
    out_specs = (
        P("group", "fsdp", "tp"),
        P("fsdp", None, "tp"),
        P("fsdp", None, "tp"),
        P("fsdp", None, "tp"),
    )
    return jax.shard_map(
        on_device, mesh=mesh, in_specs=in_specs, out_specs=out_specs, check_vma=False
    )
```

```python
import functools
import math

import jax
import jax.numpy as jnp
from jax import lax
from jax.experimental import pallas as pl
from jax.experimental.pallas import tpu as pltpu
from jax.sharding import PartitionSpec as P

D = 8192
HD = 128
STEPS = 2
OPT_STEP = 100

first_decay = 0.9
second_decay = 0.95
learn_rate = 0.15
weight_decay = 0.1
small_term = 1e-08

N_TP = 8
N_FSDP = 16
SPAN = 16
MASKED = -1e30
OFFSETS = (0, -1, 1, -2, 2, -3, 3, 4)
HID_PARTS = (
    (0, None), (1, None), (2, None), (3, None), (4, None),
    (5, None), (6, None), (7, 0), (7, 1),
)
SAME_CORE = [list(range(0, N_FSDP, 2)), list(range(1, N_FSDP, 2))]


def sibling(block, group):
    pairs = [(group * N_FSDP + f, group * N_FSDP + (f ^ 1)) for f in range(N_FSDP)]
    return lax.ppermute(block, ("group", "fsdp"), pairs)


def along_z(block, group, step):
    pairs = [(group * N_TP + z, group * N_TP + (z + step) % N_TP) for z in range(N_TP)]
    return lax.ppermute(block, ("group", "tp"), pairs)


def final_kernel(place, *refs):
    count = N_TP + 1
    hids, refs = refs[: len(HID_PARTS)], refs[len(HID_PARTS) :]
    w, w_other, queries, cache, reach_of = refs[:5]
    cots, refs = refs[5 : 5 + count], refs[5 + count :]
    cot_other, old, out = refs[:3]
    (
        hid_v, w_v, q_v, c_v, fresh_v, out_v, limit_v, score_v, cot_v, old_v,
        hid_sem, w_sem, q_sem, c_sem, out_sem, cot_sem, old_sem,
    ) = refs[3:]
    tokens, features = q_v.shape
    half = tokens // 2
    heads = features // HD
    per = 8

    @pl.when(place[0] == 0)
    def _():
        z, core = place[1], place[2]
        loads = [pltpu.make_async_copy(old, old_v, old_sem)]
        for i in range(count):
            if i < N_TP - 1:
                rows = cot_v.at[i, pl.ds(0, HD)]
            else:
                rows = cot_v.at[N_TP - 1, pl.ds((i - N_TP + 1) * 64, 64)]
            loads.append(
                pltpu.make_async_copy(cots[i].at[:, pl.ds(0, tokens)], rows, cot_sem.at[i])
            )
        loads.append(
            pltpu.make_async_copy(cot_other, cot_v.at[:, pl.ds(HD, HD)], cot_sem.at[count])
        )
        for load in loads:
            load.start()
        for load in loads:
            load.wait()
        stores = []
        for first in range(0, tokens, 128):
            at = slice(first, first + 128)
            total = None
            for r, offset in enumerate(OFFSETS):
                plane = lax.rem(z + (offset + N_TP), N_TP)
                rows = jnp.concatenate(
                    [old_v[2 * plane + core], old_v[2 * plane + 1 - core]], axis=0
                )
                part = lax.dot_general(
                    cot_v[r, :, at],
                    rows,
                    (((0,), (0,)), ((), ())),
                    preferred_element_type=jnp.float32,
                )
                total = part if total is None else total + part
            out_v[at] = (total * (1.0 / math.sqrt(D))).astype(jnp.bfloat16)
            rows = pl.ds(first, 128)
            store = pltpu.make_async_copy(out_v.at[rows], out.at[rows], out_sem.at[first // 128])
            store.start()
            stores.append(store)
        for store in stores:
            store.wait()

    @pl.when(place[0] != 0)
    def _():
        z, core = place[1], place[2]
        loads = [
            pltpu.make_async_copy(v, w_v.at[i], w_sem.at[i]) for i, v in enumerate((w, w_other))
        ]
        for i, (r, part) in enumerate(HID_PARTS):
            to = hid_v.at[r] if part is None else hid_v.at[r, pl.ds(part * half, half)]
            loads.append(pltpu.make_async_copy(hids[i], to, hid_sem.at[i]))
        loads.append(pltpu.make_async_copy(queries, q_v, q_sem))
        loads.append(pltpu.make_async_copy(cache, c_v, c_sem))
        *loads, query_load, cache_load = loads
        started = 6
        for load in (query_load, cache_load, *loads[:started]):
            load.start()
        query_load.wait()
        cache_load.wait()

        width = 128 + SPAN
        root = 1.0 / math.sqrt(HD)
        key_at = lax.broadcasted_iota(jnp.int32, (width, heads * SPAN), 0)
        token = lax.broadcasted_iota(jnp.int32, (width, heads * SPAN), 1) % SPAN
        new = key_at - 128
        owner = jnp.where(key_at < 128, key_at // 16, new // STEPS)
        limit = jnp.where(key_at < 128, key_at % 16, 0)
        limit = jnp.where(owner == token // STEPS, jnp.where(new <= token, limit, 99), 99)
        limit_v[...] = limit.astype(jnp.float32)

        def query_of(i):
            at = slice(i * SPAN, (i + 1) * SPAN)
            return jnp.concatenate(
                [q_v[at, h * HD : (h + 1) * HD] for h in range(heads)], axis=0
            )

        def scores_of(i, keys, low, high):
            score = lax.dot_general(
                keys, query_of(i), (((1,), (1,)), ((), ())), preferred_element_type=jnp.float32
            )
            return jnp.where(limit_v[low:high] < reach_of[i : i + 1, :], score * root, MASKED)

        for i in range(tokens // SPAN):
            keys = c_v[i * 8 : (i + 1) * 8, 0].reshape(128, HD)
            score_v[i] = scores_of(i, keys, 0, 128)

        total = None
        arrived = -1
        for r, offset in enumerate(OFFSETS):
            needed = 1 + max(i for i, v in enumerate(HID_PARTS, 1) if v[0] == r)
            while arrived < needed:
                arrived += 1
                loads[arrived].wait()
                if started < len(loads):
                    loads[started].start()
                    started += 1
            plane = lax.rem(z + (offset + N_TP), N_TP)
            flipped = lax.rem(plane + 4, N_TP)
            rows = [
                v for i in range(2) for v in (w_v[i, plane, :64], w_v[i, flipped, 64:])
            ]
            part = lax.dot_general(
                hid_v[r],
                jnp.concatenate(rows, axis=0),
                (((1,), (1,)), ((), ())),
                preferred_element_type=jnp.float32,
            )
            total = part if total is None else total + part
        total = total * (1.0 / math.sqrt(D))
        for i in range(2):
            own = total[:, i * 64 : (i + 1) * 64]
            other = total[:, HD + i * 64 : HD + (i + 1) * 64]
            fresh_v[i] = jnp.where(
                core == 0,
                jnp.concatenate([own, other], axis=1),
                jnp.concatenate([other, own], axis=1),
            ).astype(jnp.bfloat16)
        stores = []
        for first in range(0, tokens // SPAN, per):
            ids = range(first, first + per)
            scores = []
            for i in ids:
                keys = fresh_v[0, i * SPAN : (i + 1) * SPAN]
                scores.append(scores_of(i, keys, 128, width))
            probs = []
            for i, score in zip(ids, scores):
                score = jnp.concatenate([score_v[i], score], axis=0)
                score = jnp.exp(score - jnp.max(score, axis=0, keepdims=True))
                inverse = 1.0 / jnp.sum(score, axis=0, keepdims=True)
                probs.append((score * inverse).astype(jnp.bfloat16))
            for i, prob in zip(ids, probs):
                at = slice(i * SPAN, (i + 1) * SPAN)
                values = c_v[i * 8 : (i + 1) * 8, 1].reshape(128, HD)
                values = jnp.concatenate([values, fresh_v[1, at]], axis=0)
                mixed = lax.dot_general(
                    prob, values, (((0,), (0,)), ((), ())), preferred_element_type=jnp.float32
                ).astype(jnp.bfloat16)
                for h in range(heads):
                    out_v[at, h * HD : (h + 1) * HD] = mixed[h * SPAN : (h + 1) * SPAN]
            rows = pl.ds(first * SPAN, per * SPAN)
            store = pltpu.make_async_copy(out_v.at[rows], out.at[rows], out_sem.at[first // per])
            store.start()
            stores.append(store)
        for store in stores:
            store.wait()


def final(place, hids, w, w_other, queries, cache, reach_of, cots, cot_other, old):
    tokens, features = queries.shape
    anywhere = pl.BlockSpec(memory_space=pl.ANY)
    in_specs = [pl.BlockSpec(memory_space=pltpu.SMEM)] + [anywhere] * (len(hids) + 4)
    in_specs += [pl.BlockSpec(memory_space=pltpu.VMEM)] + [anywhere] * (len(cots) + 2)
    return pl.pallas_call(
        final_kernel,
        in_specs=in_specs,
        out_specs=anywhere,
        out_shape=jax.ShapeDtypeStruct((tokens, features), jnp.bfloat16),
        scratch_shapes=[
            pltpu.VMEM((N_TP, tokens, features), jnp.bfloat16),
            pltpu.VMEM((2,) + w.shape, jnp.bfloat16),
            pltpu.VMEM((tokens, features), jnp.bfloat16),
            pltpu.VMEM(cache.shape, jnp.bfloat16),
            pltpu.VMEM((2, tokens, HD), jnp.bfloat16),
            pltpu.VMEM((tokens, features), jnp.bfloat16),
            pltpu.VMEM((128 + SPAN, 128), jnp.float32),
            pltpu.VMEM((tokens // SPAN, 128, 128), jnp.float32),
            pltpu.VMEM((N_TP, 2 * HD, tokens), jnp.bfloat16),
            pltpu.VMEM(old.shape, jnp.bfloat16),
            pltpu.SemaphoreType.DMA((len(HID_PARTS),)),
            pltpu.SemaphoreType.DMA((2,)),
            pltpu.SemaphoreType.DMA,
            pltpu.SemaphoreType.DMA,
            pltpu.SemaphoreType.DMA((6,)),
            pltpu.SemaphoreType.DMA((N_TP + 2,)),
            pltpu.SemaphoreType.DMA,
        ],
        compiler_params=pltpu.CompilerParams(vmem_limit_bytes=56 * 1024 * 1024),
        cost_estimate=pl.CostEstimate(
            flops=2 * tokens * D * 2 * HD, bytes_accessed=24 * 2**20, transcendentals=0
        ),
    )(place, *hids, w, w_other, queries, cache, reach_of, *cots, cot_other, old)


def split_kernel(place, cot, own, other, turned):
    @pl.when(place[0] == 0)
    def _():
        core = place[2]
        for g in range(2):
            turned[...] = cot[:, g * HD : (g + 1) * HD].T
            rows = slice(g * 64, (g + 1) * 64)
            own[rows] = turned[pl.ds(pl.multiple_of(core * 64, 64), 64)]
            other[rows] = turned[pl.ds(pl.multiple_of((1 - core) * 64, 64), 64)]


def split(place, cot):
    turned = jax.ShapeDtypeStruct((HD, cot.shape[0]), cot.dtype)
    return pl.pallas_call(
        split_kernel,
        in_specs=[
            pl.BlockSpec(memory_space=pltpu.SMEM),
            pl.BlockSpec(memory_space=pltpu.VMEM),
        ],
        out_specs=[pl.BlockSpec(memory_space=pltpu.VMEM)] * 2,
        out_shape=[turned, turned],
        scratch_shapes=[pltpu.VMEM(turned.shape, turned.dtype)],
        compiler_params=pltpu.CompilerParams(vmem_limit_bytes=8 * 1024 * 1024),
    )(place, cot)


def product_kernel(place, *refs, ids, halves, first):
    count = len(ids)
    blocks, refs = refs[: count * halves], refs[count * halves :]
    hid_own, hid_other = refs[:2]
    refs = refs[2:] if first else refs[3:]
    partial, cot_other, block_v, hid_v, out_v, block_sem, hid_sem, out_sem, cot_sem = refs
    tokens, features = hid_own.shape
    rows = HD // halves

    @pl.when(place[0] == 0)
    def _():
        z = place[1]
        loads = [
            pltpu.make_async_copy(v, hid_v.at[pl.ds(i * tokens, tokens)], hid_sem.at[i])
            for i, v in enumerate((hid_own, hid_other))
        ]
        stores = []
        for i, block in enumerate(blocks):
            at = pl.ds(i * rows, rows)
            loads.append(pltpu.make_async_copy(block, block_v.at[at], block_sem.at[i]))
            part = cot_other.at[i // halves, pl.ds(i % halves * rows, rows)]
            stores.append(
                pltpu.make_async_copy(block.at[:, pl.ds(tokens, tokens)], part, cot_sem.at[i])
            )
        for copy in loads + stores:
            copy.start()
        for load in loads:
            load.wait()
        for n in range(0, features, 256):
            part = jnp.dot(
                block_v[...], hid_v[:, n : n + 256], preferred_element_type=jnp.float32
            )
            out_v[:, n : n + 256] = part.astype(jnp.bfloat16)
        for i, r in enumerate(ids):
            plane = lax.rem(z + (OFFSETS[r] + N_TP), N_TP)
            store = pltpu.make_async_copy(
                out_v.at[pl.ds(i * HD, HD)], partial.at[plane], out_sem.at[i]
            )
            store.start()
            stores.append(store)
        for store in stores:
            store.wait()


def product(place, ids, blocks, hid_own, hid_other, *before):
    first = not before
    tokens, features = hid_own.shape
    operands = (place, *blocks, hid_own, hid_other, *before)
    rows = len(ids) * HD
    return pl.pallas_call(
        functools.partial(
            product_kernel, ids=ids, halves=len(blocks) // len(ids), first=first
        ),
        in_specs=[pl.BlockSpec(memory_space=pltpu.SMEM)]
        + [pl.BlockSpec(memory_space=pl.ANY)] * (len(operands) - 1),
        out_specs=[pl.BlockSpec(memory_space=pl.ANY)] * 2,
        out_shape=[
            jax.ShapeDtypeStruct((N_TP, HD, features), jnp.bfloat16),
            jax.ShapeDtypeStruct((len(ids), HD, tokens), jnp.bfloat16),
        ],
        input_output_aliases={} if first else {len(operands) - 1: 0},
        scratch_shapes=[
            pltpu.VMEM((rows, 2 * tokens), jnp.bfloat16),
            pltpu.VMEM((2 * tokens, features), jnp.bfloat16),
            pltpu.VMEM((rows, features), jnp.bfloat16),
            pltpu.SemaphoreType.DMA((len(blocks),)),
            pltpu.SemaphoreType.DMA((2,)),
            pltpu.SemaphoreType.DMA((len(ids),)),
            pltpu.SemaphoreType.DMA((len(blocks),)),
        ],
        compiler_params=pltpu.CompilerParams(vmem_limit_bytes=16 * 1024 * 1024),
        cost_estimate=pl.CostEstimate(
            flops=4 * rows * tokens * features, bytes_accessed=12 * 2**20, transcendentals=0
        ),
    )(*operands)


def adam(gradient, master, moment1, moment2):
    new_first = first_decay * moment1 + (1.0 - first_decay) * gradient
    new_second = second_decay * moment2 + (1.0 - second_decay) * gradient * gradient
    first_hat = new_first / (1.0 - first_decay**OPT_STEP)
    second_hat = new_second / (1.0 - second_decay**OPT_STEP)
    new_master = master - learn_rate * (
        first_hat / (jnp.sqrt(second_hat) + small_term) + weight_decay * master
    )
    return new_master, new_first, new_second


def adam_kernel(place, gradient, mirrored, master, moment1, moment2, *outs):
    chosen = jnp.where(place[0] == 0, gradient[...], mirrored[...])
    for out, value in zip(outs, adam(chosen, master[...], moment1[...], moment2[...])):
        out[...] = value


def adam_outputs(place, *arrays):
    return pl.pallas_call(
        adam_kernel,
        in_specs=[pl.BlockSpec(memory_space=pltpu.SMEM)]
        + [pl.BlockSpec(memory_space=pltpu.VMEM)] * 5,
        out_specs=[pl.BlockSpec(memory_space=pltpu.VMEM)] * 3,
        out_shape=[jax.ShapeDtypeStruct(arrays[0].shape, jnp.float32)] * 3,
        compiler_params=pltpu.CompilerParams(vmem_limit_bytes=16 * 1024 * 1024),
    )(place, *arrays)


def after(block, *others):
    return lax.optimization_barrier((block, *others))[0]


def on_device(hidden, cotangent, queries, kv_cache, lengths, master, moment1, moment2):
    half_index = lax.axis_index("group")
    z = lax.axis_index("tp")
    f = lax.axis_index("fsdp")
    core = f % 2
    rows_in = hidden[0]
    tokens, features = rows_in.shape
    half = tokens // 2
    scale = 1.0 / math.sqrt(D)

    place = jnp.stack([half_index, z, core]).astype(jnp.int32)

    own, other = split(place, cotangent.reshape(tokens, 2 * HD))
    cot = jnp.concatenate([own, sibling(other, 0)], axis=1)

    cots = [cot]
    own_hidden = after(rows_in, cot)
    hids = [rows_in]
    h_up, h_down = along_z(own_hidden, 1, 1), along_z(own_hidden, 1, -1)
    up, down = along_z(cot, 0, 1), along_z(cot, 0, -1)
    cots += [up, down]
    hid_other = sibling(after(rows_in, up, down), 0)
    up, down = along_z(up, 0, 1), along_z(down, 0, -1)
    cots += [up, down]
    up, down = after(up, h_up, h_down), after(down, h_up, h_down)
    hids += [h_up, h_down]
    h_up, h_down = along_z(h_up, 1, 1), along_z(h_down, 1, -1)
    far_up, far_down = along_z(up[:64], 0, 2), along_z(down[64:], 0, -2)
    up, down = along_z(up, 0, 1), along_z(down, 0, -1)
    cots += [up, down]
    partial, others = product(place, (0, 1, 2, 3, 4), cots[:5], rows_in, hid_other)
    partial, more = product(place, (5, 6), cots[5:], rows_in, hid_other, partial)
    old = jnp.transpose(master, (1, 0, 2)).astype(jnp.bfloat16).reshape(128, features)
    old = lax.all_gather(old, "fsdp", axis=0)
    partial, up, down, old = lax.optimization_barrier((partial, far_up, far_down, old))
    partial, last = product(place, (7,), (up, down), rows_in, hid_other, partial)
    cots += [up, down]
    gathered = lax.all_to_all(partial, "fsdp", 0, 0, axis_index_groups=SAME_CORE)
    gradient = jnp.sum(gathered.astype(jnp.float32), axis=0) * scale
    gradient = jnp.transpose(gradient.reshape(2, 64, features), (1, 0, 2))

    serving = jnp.transpose(adam(gradient, master, moment1, moment2)[0], (1, 0, 2)).astype(jnp.bfloat16)
    serving = serving.reshape(128, features)
    serving, h_up, h_down = lax.optimization_barrier((serving, h_up, h_down))
    hids += [h_up, h_down]
    h_up, h_down = along_z(h_up, 1, 1), along_z(h_down, 1, -1)

    def across(rows, flip):
        pairs = [
            ((p * 2 + c) * N_TP + plane, (N_FSDP + (plane ^ flip) * 2 + c) * N_TP + p)
            for p in range(8)
            for c in range(2)
            for plane in range(N_TP)
        ]
        return lax.ppermute(rows, ("group", "fsdp", "tp"), pairs)

    keys, values = across(serving[:64], 0), across(serving[64:], 4)
    hids += [h_up, h_down]
    far_first, far_second = along_z(h_up[:half], 1, 1), along_z(h_down[half:], 1, -1)
    hids += [far_first, far_second]
    cot_other = jnp.concatenate([others, more, last], axis=0)
    keys, values, cot_other = lax.optimization_barrier((keys, values, cot_other))
    pieces = jnp.concatenate([keys, values], axis=0)
    w = lax.all_to_all(
        jnp.broadcast_to(pieces[None], (8,) + pieces.shape),
        "fsdp",
        0,
        0,
        axis_index_groups=SAME_CORE,
    )
    cot_other = sibling(cot_other, 0)
    reach_of = jnp.repeat(lengths.astype(jnp.float32).reshape(-1, 8), STEPS, axis=1)
    reach_of = jnp.tile(reach_of, (1, queries.shape[1] // HD))
    w, reach_of, gradient, far_first, far_second, cot_other = lax.optimization_barrier(
        (w, reach_of, gradient, far_first, far_second, cot_other)
    )
    hids[-2:] = [far_first, far_second]
    mirrored = lax.ppermute(gradient, "group", [(0, 1)])
    w_other = lax.ppermute(w, "fsdp", [(i, i ^ 1) for i in range(N_FSDP)])
    block = final(place, hids, w, w_other, queries, kv_cache, reach_of, cots, cot_other, old)
    mirrored, block = lax.optimization_barrier((mirrored, block))
    outs = adam_outputs(place, gradient, mirrored, master, moment1, moment2)
    return (block[None], *outs)


def solution(mesh):
    in_specs = (
        P("group", "fsdp", "tp"),
        P("fsdp", None, "tp"),
        P("fsdp", "tp"),
        P("fsdp", None, None, "tp"),
        P("fsdp"),
        P("fsdp", None, "tp"),
        P("fsdp", None, "tp"),
        P("fsdp", None, "tp"),
    )
    out_specs = (
        P("group", "fsdp", "tp"),
        P("fsdp", None, "tp"),
        P("fsdp", None, "tp"),
        P("fsdp", None, "tp"),
    )
    return jax.shard_map(
        on_device, mesh=mesh, in_specs=in_specs, out_specs=out_specs, check_vma=False
    )
```
